32 devices in a mesh: groups: 2 (over y), wide: 4 (over z), narrow: 4 (over x, core).
Axes of the slice: x: 2, y: 2, z: 4, core: 2. Of those that a mesh axis runs over, the one named last changes fastest.
Arguments:
- picture_vectors: bfloat16 [512, 768], P(('groups', 'wide', 'narrow')), parts along dimension 0, may hold values from -0.24 to 0.24
- caption_vectors: bfloat16 [512, 768], P(('groups', 'wide', 'narrow')), parts along dimension 0, may hold values from -0.24 to 0.24
- matching_caption_index: int32 [512], P(('groups', 'wide', 'narrow')), parts along dimension 0, may hold values from 0 to 255, as said below
- sharpness_array: float32 [1], replicated, may hold values from 5 to 15
- offset_term: float32 [1], replicated, may hold values from -6 to -3
Outputs:
- image_grad: float32 [512, 768], P(('groups', 'wide', 'narrow')), parts along dimension 0
- text_grad: float32 [512, 768], P(('groups', 'wide', 'narrow')), parts along dimension 0
- summary_outputs: float32 [6], P('groups'), parts along dimension 0
The draws below stay inside these ranges and needn't reach their ends.
There are 2 independent parts, one for each index of `groups`. The reference program is written for one: setup_inputs(seed, part) draws one part's arguments, and reference() takes and returns one part's arrays. A program takes and returns all parts, laid end to end along the dimension named above; an argument that names none is the same for every part. Nothing has to cross between parts.
Inputs may be any that keep to these rules, and one draw needn't show every extreme that they name: `matching_caption_index`: partner is a permutation of the 256 text indices of the group.
All inputs are finite; a program needn't handle non-finite values.
Results may differ from the reference program's by a relative error of at most 0.00082.
Values may be sent and summed in bfloat16 or wider, within the bound.
No kernel may reach another device: no remote copies, remote signals or barrier semaphores. Data moves between devices by JAX's collectives and lax.ppermute only.
A program may use at most 64 MiB of HBM per device.

```python
import math
import jax
import jax.numpy as jnp
from jax import lax

D = 768
GROUP_MATCHES = 256


def shared_parts(key):
    order = jax.random.permutation(jax.random.fold_in(key, 11), GROUP_MATCHES).astype(jnp.int32)
    base = jax.random.normal(jax.random.fold_in(key, 12), (GROUP_MATCHES, D), jnp.float32)
    flips = jax.random.bernoulli(jax.random.fold_in(key, 13), 0.5, (D,))
    signs = jnp.where(flips, 1.0, -1.0).astype(jnp.float32)
    return (order, base, signs)


def draw_matching_caption_index(key, part):
    order, base, signs = shared_parts(key)
    return order


def draw_picture_vectors(key, part):
    order, base, signs = shared_parts(key)
    key = jax.random.fold_in(key, 1)
    place = jnp.arange(GROUP_MATCHES, dtype=jnp.float32) / GROUP_MATCHES
    rough = jnp.exp(jax.random.uniform(jax.random.fold_in(key, 2), (GROUP_MATCHES, 1), jnp.float32, math.log(0.6), math.log(1.6)))
    ramp = 0.2 + 0.7 * place
    weight = ramp[:, None] * rough
    rows = 0.04 * (base + weight * signs[None, :])
    return jnp.clip(rows, -0.24, 0.24).astype(jnp.bfloat16)


def draw_caption_vectors(key, part):
    order, base, signs = shared_parts(key)
    key = jax.random.fold_in(key, 2)
    inverse = jnp.zeros((GROUP_MATCHES,), jnp.int32).at[order].set(jnp.arange(GROUP_MATCHES, dtype=jnp.int32))
    own = jax.random.normal(jax.random.fold_in(key, 1), (GROUP_MATCHES, D), jnp.float32)
    share = jnp.exp(jax.random.uniform(jax.random.fold_in(key, 2), (GROUP_MATCHES, 1), jnp.float32, math.log(0.4), 0.0))
    rows = 0.04 * (0.8 * base[inverse] + 0.6 * own + share * signs[None, :])
    return jnp.clip(rows, -0.24, 0.24).astype(jnp.bfloat16)


def setup_inputs(seed: int = 0, part: int = 0) -> dict:
    keys = jax.random.split(jax.random.key(seed), 6)
    own_keys = jax.random.split(jax.random.fold_in(keys[5], part), 6)
    return {
        "picture_vectors": draw_picture_vectors(jax.random.fold_in(jax.random.fold_in(keys[5], part), 71), part),
        "caption_vectors": draw_caption_vectors(jax.random.fold_in(jax.random.fold_in(keys[5], part), 71), part),
        "matching_caption_index": draw_matching_caption_index(jax.random.fold_in(jax.random.fold_in(keys[5], part), 71), part),
        "sharpness_array": jnp.clip(jax.random.uniform(keys[3], (1,), jnp.float32, 5.0, 15.0), 5.0, 15.0),
        "offset_term": jnp.clip(jax.random.uniform(keys[4], (1,), jnp.float32, -6.0, -3.0), -6.0, -3.0),
    }


def normalize(rows):
    values = rows.astype(jnp.float32)
    scales = lax.rsqrt(lax.optimization_barrier(jnp.sum(values * values, axis=1, keepdims=True)) + 1e-06)
    return (values * scales, scales)

def reference(picture_vectors, caption_vectors, matching_caption_index, sharpness_array, offset_term):
    unit_img, inv_img = normalize(picture_vectors)
    normalized_text_rows, inv_txt = normalize(caption_vectors)
    img_half = unit_img.astype(jnp.bfloat16)
    txt_half = normalized_text_rows.astype(jnp.bfloat16)
    sharpness_factor = sharpness_array[0]
    shift = offset_term[0]
    block = math.gcd(GROUP_MATCHES, 512)
    count = GROUP_MATCHES // block
    columns = jnp.arange(GROUP_MATCHES, dtype=jnp.int32)
    img_blocks = img_half.reshape(count, block, D)
    paired_block_list = matching_caption_index.reshape(count, block)

    def step(carry, item):
        txt_acc, loss_acc, temp_acc, bias_acc = carry
        rows, mates = item
        cosine = jnp.dot(rows, txt_half.T, preferred_element_type=jnp.float32)
        logit = sharpness_factor * cosine + shift
        sign = jnp.where(mates[:, None] == columns[None, :], 1.0, -1.0).astype(jnp.float32)
        loss_acc = loss_acc + jnp.sum(jax.nn.softplus(-sign * logit))
        slope = -sign * jax.nn.sigmoid(-sign * logit)
        temp_acc = temp_acc + jnp.sum(slope * cosine)
        bias_acc = bias_acc + jnp.sum(slope)
        weighted = (sharpness_factor * slope).astype(jnp.bfloat16)
        img_part = jnp.dot(weighted, txt_half, preferred_element_type=jnp.float32)
        txt_acc = txt_acc + jnp.dot(weighted.T, rows, preferred_element_type=jnp.float32)
        return ((txt_acc, loss_acc, temp_acc, bias_acc), img_part)
    start = (jnp.zeros((GROUP_MATCHES, D), jnp.float32), jnp.float32(0.0), jnp.float32(0.0), jnp.float32(0.0))
    finished_outcome, img_parts = lax.scan(step, start, (img_blocks, paired_block_list))
    caption_derivative_on_sphere, objective_total, sharpness_derivative, offset_derivative_total = finished_outcome
    img_grad_unit = img_parts.reshape(GROUP_MATCHES, D)
    image_grad = inv_img * (img_grad_unit - unit_img * lax.optimization_barrier(jnp.sum(unit_img * img_grad_unit, axis=1, keepdims=True)))
    text_grad = inv_txt * (caption_derivative_on_sphere - normalized_text_rows * lax.optimization_barrier(jnp.sum(normalized_text_rows * caption_derivative_on_sphere, axis=1, keepdims=True)))
    summary_outputs = jnp.stack([objective_total / GROUP_MATCHES, sharpness_derivative, offset_derivative_total]).astype(jnp.float32)
    return (image_grad, text_grad, summary_outputs)
```

```python
import jax
import jax.numpy as jnp
from jax import lax
from jax.experimental import pallas as pl
from jax.experimental.pallas import tpu as pltpu
from jax.sharding import PartitionSpec as P

GROUP = ("wide", "narrow")
LANES = 128
VMEM = pl.BlockSpec(memory_space=pltpu.VMEM)
SMEM = pl.BlockSpec(memory_space=pltpu.SMEM)


def normalize(rows):
    values = rows.astype(jnp.float32)
    scales = lax.rsqrt(jnp.sum(values * values, axis=1, keepdims=True) + 1e-06)
    return (values * scales, scales)


def backnorm(unit, scales, grad_unit):
    return scales * (grad_unit - unit * jnp.sum(unit * grad_unit, axis=1, keepdims=True))


def pair_terms(cosine, logit, matched):
    against = jnp.where(matched, -logit, logit)
    small = jnp.exp(-jnp.abs(logit))
    loss = jnp.maximum(against, 0.0) + jnp.log1p(small)
    sigma = jnp.where(against >= 0.0, 1.0, small) / (1.0 + small)
    return loss, jnp.where(matched, -sigma, sigma)


def pack_kernel(mates_ref, img_ref, txt_ref, out_ref):
    rows, width = img_ref.shape
    tiles = width // LANES
    for t in range(tiles):
        out_ref[t] = img_ref[:, t * LANES : (t + 1) * LANES]
        out_ref[tiles + t] = txt_ref[:, t * LANES : (t + 1) * LANES]
    row = lax.broadcasted_iota(jnp.int32, (rows, LANES), 0)
    mates = jnp.zeros((rows, LANES), jnp.int32)
    for r in range(rows):
        mates = jnp.where(row == r, mates_ref[r], mates)
    out_ref[2 * tiles] = mates.astype(jnp.float32).astype(jnp.bfloat16)


def pair_kernel(distances, narrow, sharp_ref, shift_ref, *refs):
    blocks = refs[: len(distances)]
    image_out, text_out, summary_out, img_half, txt_half, mates, weights = refs[len(distances) :]
    count = len(distances)
    rows, width = image_out.shape
    tiles = width // LANES
    total = rows * count
    me = lax.axis_index("wide") * narrow + lax.axis_index("narrow")
    sharp, shift = sharp_ref[0], shift_ref[0]

    def unit_tiles(block, first):
        values = [block[first + t].astype(jnp.float32) for t in range(tiles)]
        squares = values[0] * values[0]
        for v in values[1:]:
            squares = squares + v * v
        scales = lax.rsqrt(jnp.sum(squares, axis=1, keepdims=True) + 1e-06)
        return [v * scales for v in values], scales

    own = None
    for distance, block in zip(distances, blocks):
        here = pl.ds(pl.multiple_of((me ^ distance) * rows, rows), rows)
        img_units, img_scale = unit_tiles(block, 0)
        txt_units, txt_scale = unit_tiles(block, tiles)
        for t in range(tiles):
            lanes = slice(t * LANES, (t + 1) * LANES)
            img_half[here, lanes] = img_units[t].astype(jnp.bfloat16)
            txt_half[here, lanes] = txt_units[t].astype(jnp.bfloat16)
        mates[here, :] = block[2 * tiles].astype(jnp.float32)
        if distance == 0:
            own = (img_units, img_scale, txt_units, txt_scale)

    nt = (((1,), (1,)), ((), ()))
    cosine = lax.dot_general(img_half[...], txt_half[...], nt, preferred_element_type=jnp.float32)
    logit = sharp * cosine + shift
    column = lax.broadcasted_iota(jnp.int32, (total, LANES), 1).astype(jnp.float32)
    matched = jnp.concatenate(
        [mates[...] == column + float(c * LANES) for c in range(total // LANES)], axis=1
    )
    loss, slope = pair_terms(cosine, logit, matched)
    summary_out[0] = jnp.sum(loss) / total
    summary_out[1] = jnp.sum(slope * cosine)
    summary_out[2] = jnp.sum(slope)
    weights[...] = (sharp * slope).astype(jnp.bfloat16)

    mine = pl.ds(pl.multiple_of(me * rows, rows), rows)
    picked = (
        lax.broadcasted_iota(jnp.int32, (rows, total), 1)
        == lax.broadcasted_iota(jnp.int32, (rows, total), 0) + me * rows
    )
    text_weights = lax.dot_general(
        picked.astype(jnp.float32).astype(jnp.bfloat16),
        weights[...],
        nt,
        preferred_element_type=jnp.float32,
    ).astype(jnp.bfloat16)
    img_grad = jnp.dot(weights[mine, :], txt_half[...], preferred_element_type=jnp.float32)
    txt_grad = jnp.dot(text_weights, img_half[...], preferred_element_type=jnp.float32)

    def store(out, units, scale, grad):
        parts = [grad[:, t * LANES : (t + 1) * LANES] for t in range(tiles)]
        along = units[0] * parts[0]
        for u, g in zip(units[1:], parts[1:]):
            along = along + u * g
        along = jnp.sum(along, axis=1, keepdims=True)
        for t in range(tiles):
            out[:, t * LANES : (t + 1) * LANES] = scale * (parts[t] - units[t] * along)

    store(image_out, own[0], own[1], img_grad)
    store(text_out, own[2], own[3], txt_grad)


def small_group(wide, narrow, images, texts, mates, sharpness, offset):
    rows, width = images.shape
    count = wide * narrow
    tiles = 2 * (width // LANES) + 1
    packed = pl.pallas_call(
        pack_kernel,
        out_shape=jax.ShapeDtypeStruct((tiles, rows, LANES), jnp.bfloat16),
        in_specs=[SMEM, VMEM, VMEM],
        out_specs=VMEM,
    )(mates, images, texts)

    def swap(x, distance):
        return lax.ppermute(x, GROUP, [(i, i ^ distance) for i in range(count)])

    held = {0: packed}
    bit = narrow
    held[2 * bit] = swap(packed, 2 * bit)
    held[bit] = swap(packed, bit)
    held[3 * bit] = swap(held[2 * bit], bit)
    for bit in (2, 1):
        for distance in list(held):
            held[distance + bit] = swap(held[distance], bit)

    distances = tuple(held)
    total = rows * count
    kernel = lambda *refs: pair_kernel(distances, narrow, *refs)
    return pl.pallas_call(
        kernel,
        out_shape=(
            jax.ShapeDtypeStruct((rows, width), jnp.float32),
            jax.ShapeDtypeStruct((rows, width), jnp.float32),
            jax.ShapeDtypeStruct((3,), jnp.float32),
        ),
        in_specs=[SMEM, SMEM] + [VMEM] * count,
        out_specs=(VMEM, VMEM, SMEM),
        scratch_shapes=[
            pltpu.VMEM((total, width), jnp.bfloat16),
            pltpu.VMEM((total, width), jnp.bfloat16),
            pltpu.VMEM((total, LANES), jnp.float32),
            pltpu.VMEM((total, total), jnp.bfloat16),
        ],
        compiler_params=pltpu.CompilerParams(vmem_limit_bytes=32 * 1024 * 1024),
    )(sharpness, offset, *held.values())


def any_group(wide, narrow, images, texts, mates, sharpness, offset):
    rows = images.shape[0]
    total = rows * wide * narrow
    first = (lax.axis_index("wide") * narrow + lax.axis_index("narrow")) * rows
    unit_img, inv_img = normalize(images)
    unit_txt, inv_txt = normalize(texts)
    img_half, txt_half = unit_img.astype(jnp.bfloat16), unit_txt.astype(jnp.bfloat16)
    all_img = lax.all_gather(img_half, GROUP, axis=0, tiled=True)
    all_txt = lax.all_gather(txt_half, GROUP, axis=0, tiled=True)
    all_mates = lax.all_gather(mates, GROUP, axis=0, tiled=True)
    sharp, shift = sharpness[0], offset[0]

    def weigh(cosine, matched):
        loss, slope = pair_terms(cosine, sharp * cosine + shift, matched)
        return loss, slope, (sharp * slope).astype(jnp.bfloat16)

    here = first + jnp.arange(rows, dtype=jnp.int32)
    there = jnp.arange(total, dtype=jnp.int32)
    cosine = jnp.dot(img_half, all_txt.T, preferred_element_type=jnp.float32)
    loss, slope, weighted = weigh(cosine, mates[:, None] == there[None, :])
    sums = jnp.stack([jnp.sum(loss) / total, jnp.sum(slope * cosine), jnp.sum(slope)])
    img_grad = jnp.dot(weighted, all_txt, preferred_element_type=jnp.float32)
    turned = jnp.dot(txt_half, all_img.T, preferred_element_type=jnp.float32)
    weighted = weigh(turned, all_mates[None, :] == here[:, None])[2]
    txt_grad = jnp.dot(weighted, all_img, preferred_element_type=jnp.float32)
    return (
        backnorm(unit_img, inv_img, img_grad),
        backnorm(unit_txt, inv_txt, txt_grad),
        lax.psum(sums, GROUP),
    )


def solution(mesh):
    wide, narrow = mesh.shape["wide"], mesh.shape["narrow"]

    def per_device(images, texts, mates, sharpness, offset):
        total = images.shape[0] * wide * narrow
        small = wide == 4 and narrow == 4 and total <= 256 and total % LANES == 0
        form = small_group if small else any_group
        return form(wide, narrow, images, texts, mates, sharpness, offset)

    rows = P(("groups", "wide", "narrow"))
    return jax.shard_map(
        per_device,
        mesh=mesh,
        in_specs=(rows, rows, rows, P(), P()),
        out_specs=(rows, rows, P("groups")),
        check_vma=False,
    )
```

```python
import jax
import jax.numpy as jnp
from jax import lax
from jax.experimental import pallas as pl
from jax.experimental.pallas import tpu as pltpu
from jax.sharding import PartitionSpec as P

GROUP = ("wide", "narrow")
LANES = 128
VMEM = pl.BlockSpec(memory_space=pltpu.VMEM)
SMEM = pl.BlockSpec(memory_space=pltpu.SMEM)
HBM = pl.BlockSpec(memory_space=pltpu.HBM)


def in_hbm(x):
    return pltpu.with_memory_space_constraint(x, pltpu.HBM)


def normalize(rows):
    values = rows.astype(jnp.float32)
    scales = lax.rsqrt(jnp.sum(values * values, axis=1, keepdims=True) + 1e-06)
    return (values * scales, scales)


def backnorm(unit, scales, grad_unit):
    return scales * (grad_unit - unit * jnp.sum(unit * grad_unit, axis=1, keepdims=True))


def pair_terms(cosine, logit, matched):
    against = jnp.where(matched, -logit, logit)
    small = jnp.exp(-jnp.abs(logit))
    loss = jnp.maximum(against, 0.0) + jnp.log1p(small)
    sigma = jnp.where(against >= 0.0, 1.0, small) / (1.0 + small)
    return loss, jnp.where(matched, -sigma, sigma)


def pack_kernel(mates_hbm, img_hbm, txt_hbm, out_ref, mates_ref, mates_sem, sems):
    rows, width = img_hbm.shape
    tiles = width // LANES
    copies = []
    for i, source in enumerate((img_hbm, txt_hbm)):
        for t in range(tiles):
            at = i * tiles + t
            copies.append(
                pltpu.make_async_copy(
                    source.at[:, t * LANES : (t + 1) * LANES], out_ref.at[at], sems.at[at]
                )
            )
    indices = pltpu.make_async_copy(mates_hbm, mates_ref, mates_sem)
    indices.start()
    for copy in copies:
        copy.start()
    indices.wait()
    row = lax.broadcasted_iota(jnp.int32, (rows, LANES), 0)
    mates = jnp.zeros((rows, LANES), jnp.int32)
    for r in range(rows):
        mates = jnp.where(row == r, mates_ref[r], mates)
    out_ref[2 * tiles] = mates.astype(jnp.float32).astype(jnp.bfloat16)
    for copy in copies:
        copy.wait()


def pair_kernel(held, narrow, scalars_ref, *refs):
    count = sum(len(distances) for distances in held)
    stacks, refs = refs[: len(held)], refs[len(held) :]
    image_out, text_out, summary_out = refs[:3]
    img_half, txt_half, mates, weights = refs[3:]
    rows, width = image_out.shape
    tiles = width // LANES
    total = rows * count
    me = lax.axis_index("wide") * narrow + lax.axis_index("narrow")

    def unit_tiles(tile, first):
        values = [tile(first + t).astype(jnp.float32) for t in range(tiles)]
        squares = values[0] * values[0]
        for v in values[1:]:
            squares = squares + v * v
        scales = lax.rsqrt(jnp.sum(squares, axis=1, keepdims=True) + 1e-06)
        return [v * scales for v in values], scales

    own = None
    for distances, stack in zip(held, stacks):
        for place, distance in enumerate(distances):
            tile = lambda t: stack[place * (2 * tiles + 1) + t]
            here = pl.ds(pl.multiple_of((me ^ distance) * rows, rows), rows)
            img_units, img_scale = unit_tiles(tile, 0)
            txt_units, txt_scale = unit_tiles(tile, tiles)
            for t in range(tiles):
                lanes = slice(t * LANES, (t + 1) * LANES)
                img_half[here, lanes] = img_units[t].astype(jnp.bfloat16)
                txt_half[here, lanes] = txt_units[t].astype(jnp.bfloat16)
            mates[here, :] = tile(2 * tiles).astype(jnp.float32)
            if distance == 0:
                own = (img_units, img_scale, txt_units, txt_scale)

    nt = (((1,), (1,)), ((), ()))
    cosine = lax.dot_general(img_half[...], txt_half[...], nt, preferred_element_type=jnp.float32)
    sharp, shift = scalars_ref[0:1, :], scalars_ref[1:2, :]
    logit = sharp * cosine + shift
    column = lax.broadcasted_iota(jnp.int32, (total, LANES), 1).astype(jnp.float32)
    matched = jnp.concatenate(
        [mates[...] == column + float(c * LANES) for c in range(total // LANES)], axis=1
    )
    loss, slope = pair_terms(cosine, logit, matched)
    summary_out[0] = jnp.sum(loss) / total
    summary_out[1] = jnp.sum(slope * cosine)
    summary_out[2] = jnp.sum(slope)
    weights[...] = (sharp * slope).astype(jnp.bfloat16)

    mine = pl.ds(pl.multiple_of(me * rows, rows), rows)
    picked = (
        lax.broadcasted_iota(jnp.int32, (rows, total), 1)
        == lax.broadcasted_iota(jnp.int32, (rows, total), 0) + me * rows
    )
    text_weights = lax.dot_general(
        picked.astype(jnp.float32).astype(jnp.bfloat16),
        weights[...],
        nt,
        preferred_element_type=jnp.float32,
    ).astype(jnp.bfloat16)
    img_grad = jnp.dot(weights[mine, :], txt_half[...], preferred_element_type=jnp.float32)
    txt_grad = jnp.dot(text_weights, img_half[...], preferred_element_type=jnp.float32)

    def store(out, units, scale, grad):
        parts = [grad[:, t * LANES : (t + 1) * LANES] for t in range(tiles)]
        along = units[0] * parts[0]
        for u, g in zip(units[1:], parts[1:]):
            along = along + u * g
        along = jnp.sum(along, axis=1, keepdims=True)
        for t in range(tiles):
            out[:, t * LANES : (t + 1) * LANES] = scale * (parts[t] - units[t] * along)

    store(image_out, own[0], own[1], img_grad)
    store(text_out, own[2], own[3], txt_grad)


def small_group(wide, narrow, images, texts, mates, sharpness, offset):
    rows, width = images.shape
    count = wide * narrow
    tiles = 2 * (width // LANES) + 1
    packed = pl.pallas_call(
        pack_kernel,
        out_shape=pltpu.VMEM((tiles, rows, LANES), jnp.bfloat16),
        in_specs=[HBM, HBM, HBM],
        out_specs=VMEM,
        scratch_shapes=[
            pltpu.SMEM((rows,), jnp.int32),
            pltpu.SemaphoreType.DMA,
            pltpu.SemaphoreType.DMA((tiles - 1,)),
        ],
    )(*(in_hbm(x) for x in (mates, images, texts)))

    def swap(x, distance):
        return lax.ppermute(x, GROUP, [(i, i ^ distance) for i in range(count)])

    total = rows * count
    scalars = jnp.stack([jnp.broadcast_to(v, (total,)) for v in (sharpness, offset)])
    def join(*parts):
        return tuple(d for ds, _ in parts for d in ds), jnp.concatenate([p for _, p in parts])

    def send(part, distance):
        return tuple(d ^ distance for d in part[0]), swap(part[1], distance)

    z, x, c = narrow, 2, 1
    own = ((0,), packed)
    z3 = send(own, 3 * z)
    z2 = send(own, 2 * z)
    z1 = send(own, 1 * z)
    early, late = join(own,z2), join(z1,z3)
    xearly, xlate = send(early, x), send(late, x)
    held = [early, late, xearly, xlate]
    held += [send(h, c) for h in held]

    kernel = lambda *refs: pair_kernel([d for d, _ in held], narrow, *refs)
    return pl.pallas_call(
        kernel,
        out_shape=(
            jax.ShapeDtypeStruct((rows, width), jnp.float32),
            jax.ShapeDtypeStruct((rows, width), jnp.float32),
            jax.ShapeDtypeStruct((3,), jnp.float32),
        ),
        in_specs=[VMEM] * (1 + len(held)),
        out_specs=(VMEM, VMEM, SMEM),
        scratch_shapes=[
            pltpu.VMEM((total, width), jnp.bfloat16),
            pltpu.VMEM((total, width), jnp.bfloat16),
            pltpu.VMEM((total, LANES), jnp.float32),
            pltpu.VMEM((total, total), jnp.bfloat16),
        ],
        compiler_params=pltpu.CompilerParams(vmem_limit_bytes=32 * 1024 * 1024),
    )(scalars, *[x for _, x in held])


def any_group(wide, narrow, images, texts, mates, sharpness, offset):
    rows = images.shape[0]
    total = rows * wide * narrow
    first = (lax.axis_index("wide") * narrow + lax.axis_index("narrow")) * rows
    unit_img, inv_img = normalize(images)
    unit_txt, inv_txt = normalize(texts)
    img_half, txt_half = unit_img.astype(jnp.bfloat16), unit_txt.astype(jnp.bfloat16)
    all_img = lax.all_gather(img_half, GROUP, axis=0, tiled=True)
    all_txt = lax.all_gather(txt_half, GROUP, axis=0, tiled=True)
    all_mates = lax.all_gather(mates, GROUP, axis=0, tiled=True)
    sharp, shift = sharpness[0], offset[0]

    def weigh(cosine, matched):
        loss, slope = pair_terms(cosine, sharp * cosine + shift, matched)
        return loss, slope, (sharp * slope).astype(jnp.bfloat16)

    here = first + jnp.arange(rows, dtype=jnp.int32)
    there = jnp.arange(total, dtype=jnp.int32)
    cosine = jnp.dot(img_half, all_txt.T, preferred_element_type=jnp.float32)
    loss, slope, weighted = weigh(cosine, mates[:, None] == there[None, :])
    sums = jnp.stack([jnp.sum(loss) / total, jnp.sum(slope * cosine), jnp.sum(slope)])
    img_grad = jnp.dot(weighted, all_txt, preferred_element_type=jnp.float32)
    turned = jnp.dot(txt_half, all_img.T, preferred_element_type=jnp.float32)
    weighted = weigh(turned, all_mates[None, :] == here[:, None])[2]
    txt_grad = jnp.dot(weighted, all_img, preferred_element_type=jnp.float32)
    return (
        backnorm(unit_img, inv_img, img_grad),
        backnorm(unit_txt, inv_txt, txt_grad),
        lax.psum(sums, GROUP),
    )


def solution(mesh):
    wide, narrow = mesh.shape["wide"], mesh.shape["narrow"]

    def per_device(images, texts, mates, sharpness, offset):
        total = images.shape[0] * wide * narrow
        small = wide == 4 and narrow == 4 and total <= 256 and total % LANES == 0
        form = small_group if small else any_group
        return form(wide, narrow, images, texts, mates, sharpness, offset)

    rows = P(("groups", "wide", "narrow"))
    return jax.shard_map(
        per_device,
        mesh=mesh,
        in_specs=(rows, rows, rows, P(), P()),
        out_specs=(rows, rows, P("groups")),
        check_vma=False,
    )
```

```python
import jax
import jax.numpy as jnp
from jax import lax
from jax.experimental import pallas as pl
from jax.experimental.pallas import tpu as pltpu
from jax.sharding import PartitionSpec as P

GROUP = ("wide", "narrow")
LANES = 128
VMEM = pl.BlockSpec(memory_space=pltpu.VMEM)
SMEM = pl.BlockSpec(memory_space=pltpu.SMEM)
HBM = pl.BlockSpec(memory_space=pltpu.HBM)


def in_vmem(x):
    return pltpu.with_memory_space_constraint(x, pltpu.VMEM)


def in_hbm(x):
    return pltpu.with_memory_space_constraint(x, pltpu.HBM)


def normalize(rows):
    values = rows.astype(jnp.float32)
    scales = lax.rsqrt(jnp.sum(values * values, axis=1, keepdims=True) + 1e-06)
    return (values * scales, scales)


def backnorm(unit, scales, grad_unit):
    return scales * (grad_unit - unit * jnp.sum(unit * grad_unit, axis=1, keepdims=True))


def pair_terms(cosine, logit, matched):
    against = jnp.where(matched, -logit, logit)
    small = jnp.exp(-jnp.abs(logit))
    loss = jnp.maximum(against, 0.0) + jnp.log1p(small)
    sigma = jnp.where(against >= 0.0, 1.0, small) / (1.0 + small)
    return loss, jnp.where(matched, -sigma, sigma)


def pack_kernel(mates_hbm, img_hbm, txt_hbm, out_ref, mates_ref, mates_sem, sems):
    rows, width = img_hbm.shape
    copies = [
        pltpu.make_async_copy(source, out_ref.at[:, i * width : (i + 1) * width], sems.at[i])
        for i, source in enumerate((img_hbm, txt_hbm))
    ]
    indices = pltpu.make_async_copy(mates_hbm, mates_ref, mates_sem)
    indices.start()
    for copy in copies:
        copy.start()
    indices.wait()
    row = lax.broadcasted_iota(jnp.int32, (rows, LANES), 0)
    mates = jnp.zeros((rows, LANES), jnp.int32)
    for r in range(rows):
        mates = jnp.where(row == r, mates_ref[r], mates)
    out_ref[:, 2 * width :] = mates.astype(jnp.float32).astype(jnp.bfloat16)
    for copy in copies:
        copy.wait()


def pair_kernel(held, extra, narrow, scalars_ref, *refs):
    count = sum(len(distances) for distances in held)
    stacks, refs = refs[: len(held)], refs[len(held) + extra :]
    image_out, text_out, summary_out = refs[:3]
    img_half, txt_half, mates, weights = refs[3:]
    rows, width = image_out.shape
    tiles = width // LANES
    total = rows * count
    me = lax.axis_index("wide") * narrow + lax.axis_index("narrow")

    def unit_tiles(tile, first):
        values = [tile(first + t).astype(jnp.float32) for t in range(tiles)]
        squares = values[0] * values[0]
        for v in values[1:]:
            squares = squares + v * v
        scales = lax.rsqrt(jnp.sum(squares, axis=1, keepdims=True) + 1e-06)
        return [v * scales for v in values], scales

    own = None
    for distances, stack in zip(held, stacks):
        for place, distance in enumerate(distances):
            tile = lambda t: stack[place * rows : (place + 1) * rows, t * LANES : (t + 1) * LANES]
            here = pl.ds(pl.multiple_of((me ^ distance) * rows, rows), rows)
            img_units, img_scale = unit_tiles(tile, 0)
            txt_units, txt_scale = unit_tiles(tile, tiles)
            for t in range(tiles):
                lanes = slice(t * LANES, (t + 1) * LANES)
                img_half[here, lanes] = img_units[t].astype(jnp.bfloat16)
                txt_half[here, lanes] = txt_units[t].astype(jnp.bfloat16)
            mates[here, :] = tile(2 * tiles).astype(jnp.float32)
            if distance == 0:
                own = (img_units, img_scale, txt_units, txt_scale)

    nt = (((1,), (1,)), ((), ()))
    cosine = lax.dot_general(img_half[...], txt_half[...], nt, preferred_element_type=jnp.float32)
    sharp, shift = scalars_ref[0:1, :], scalars_ref[1:2, :]
    logit = sharp * cosine + shift
    column = lax.broadcasted_iota(jnp.int32, (total, LANES), 1).astype(jnp.float32)
    matched = jnp.concatenate(
        [mates[...] == column + float(c * LANES) for c in range(total // LANES)], axis=1
    )
    loss, slope = pair_terms(cosine, logit, matched)
    weights[...] = (sharp * slope).astype(jnp.bfloat16)
    summary_out[0] = jnp.sum(loss) / total
    summary_out[1] = jnp.sum(slope * cosine)
    summary_out[2] = jnp.sum(slope)

    mine = pl.ds(pl.multiple_of(me * rows, rows), rows)
    picked = (
        lax.broadcasted_iota(jnp.int32, (rows, total), 1)
        == lax.broadcasted_iota(jnp.int32, (rows, total), 0) + me * rows
    )
    text_weights = lax.dot_general(
        picked.astype(jnp.float32).astype(jnp.bfloat16),
        weights[...],
        nt,
        preferred_element_type=jnp.float32,
    ).astype(jnp.bfloat16)
    img_grad = jnp.dot(weights[mine, :], txt_half[...], preferred_element_type=jnp.float32)
    txt_grad = jnp.dot(text_weights, img_half[...], preferred_element_type=jnp.float32)

    def store(out, units, scale, grad):
        parts = [grad[:, t * LANES : (t + 1) * LANES] for t in range(tiles)]
        along = units[0] * parts[0]
        for u, g in zip(units[1:], parts[1:]):
            along = along + u * g
        along = jnp.sum(along, axis=1, keepdims=True)
        for t in range(tiles):
            out[:, t * LANES : (t + 1) * LANES] = scale * (parts[t] - units[t] * along)

    store(image_out, own[0], own[1], img_grad)
    store(text_out, own[2], own[3], txt_grad)


def small_group(wide, narrow, images, texts, mates, sharpness, offset):
    rows, width = images.shape
    count = wide * narrow
    packed = pl.pallas_call(
        pack_kernel,
        out_shape=pltpu.VMEM((rows, 2 * width + LANES), jnp.bfloat16),
        in_specs=[HBM, HBM, HBM],
        out_specs=VMEM,
        scratch_shapes=[
            pltpu.SMEM((rows,), jnp.int32),
            pltpu.SemaphoreType.DMA,
            pltpu.SemaphoreType.DMA((2,)),
        ],
    )(*(in_hbm(x) for x in (mates, images, texts)))

    def swap(x, distance):
        return lax.ppermute(x, GROUP, [(i, i ^ distance) for i in range(count)])

    total = rows * count
    scalars = jnp.stack([jnp.broadcast_to(v, (total,)) for v in (sharpness, offset)])
    extras = ()
    def join(*parts):
        return tuple(d for ds, _ in parts for d in ds), jnp.concatenate([p for _, p in parts])

    def send(part, distance):
        return tuple(d ^ distance for d in part[0]), swap(part[1], distance)

    z, x, c = narrow, 2, 1
    own = ((0,), packed)
    z3 = send(own, 3 * z)
    z2 = send(own, 2 * z)
    z1 = send(own, 1 * z)
    early, late = join(own,z3), join(z1,z2)
    part, scalars = lax.optimization_barrier((early[1], scalars))
    early = (early[0], part)
    xearly, xlate = send(early, x), send(late, x)
    held = [early, late, xearly, xlate]
    held += [send(h, c) for h in held]

    kernel = lambda *refs: pair_kernel([d for d, _ in held], len(extras), narrow, *refs)
    return pl.pallas_call(
        kernel,
        out_shape=(
            jax.ShapeDtypeStruct((rows, width), jnp.float32),
            jax.ShapeDtypeStruct((rows, width), jnp.float32),
            jax.ShapeDtypeStruct((3,), jnp.float32),
        ),
        in_specs=[VMEM] * (1 + len(held) + len(extras)),
        out_specs=(VMEM, VMEM, SMEM),
        scratch_shapes=[
            pltpu.VMEM((total, width), jnp.bfloat16),
            pltpu.VMEM((total, width), jnp.bfloat16),
            pltpu.VMEM((total, LANES), jnp.float32),
            pltpu.VMEM((total, total), jnp.bfloat16),
        ],
        compiler_params=pltpu.CompilerParams(vmem_limit_bytes=32 * 1024 * 1024),
    )(scalars, *[x for _, x in held], *extras)


def any_group(wide, narrow, images, texts, mates, sharpness, offset):
    rows = images.shape[0]
    total = rows * wide * narrow
    first = (lax.axis_index("wide") * narrow + lax.axis_index("narrow")) * rows
    unit_img, inv_img = normalize(images)
    unit_txt, inv_txt = normalize(texts)
    img_half, txt_half = unit_img.astype(jnp.bfloat16), unit_txt.astype(jnp.bfloat16)
    all_img = lax.all_gather(img_half, GROUP, axis=0, tiled=True)
    all_txt = lax.all_gather(txt_half, GROUP, axis=0, tiled=True)
    all_mates = lax.all_gather(mates, GROUP, axis=0, tiled=True)
    sharp, shift = sharpness[0], offset[0]

    def weigh(cosine, matched):
        loss, slope = pair_terms(cosine, sharp * cosine + shift, matched)
        return loss, slope, (sharp * slope).astype(jnp.bfloat16)

    here = first + jnp.arange(rows, dtype=jnp.int32)
    there = jnp.arange(total, dtype=jnp.int32)
    cosine = jnp.dot(img_half, all_txt.T, preferred_element_type=jnp.float32)
    loss, slope, weighted = weigh(cosine, mates[:, None] == there[None, :])
    sums = jnp.stack([jnp.sum(loss) / total, jnp.sum(slope * cosine), jnp.sum(slope)])
    img_grad = jnp.dot(weighted, all_txt, preferred_element_type=jnp.float32)
    turned = jnp.dot(txt_half, all_img.T, preferred_element_type=jnp.float32)
    weighted = weigh(turned, all_mates[None, :] == here[:, None])[2]
    txt_grad = jnp.dot(weighted, all_img, preferred_element_type=jnp.float32)
    return (
        backnorm(unit_img, inv_img, img_grad),
        backnorm(unit_txt, inv_txt, txt_grad),
        lax.psum(sums, GROUP),
    )


def solution(mesh):
    wide, narrow = mesh.shape["wide"], mesh.shape["narrow"]

    def per_device(images, texts, mates, sharpness, offset):
        total = images.shape[0] * wide * narrow
        small = wide == 4 and narrow == 4 and total <= 256 and total % LANES == 0
        form = small_group if small else any_group
        return form(wide, narrow, images, texts, mates, sharpness, offset)

    rows = P(("groups", "wide", "narrow"))
    return jax.shard_map(
        per_device,
        mesh=mesh,
        in_specs=(rows, rows, rows, P(), P()),
        out_specs=(rows, rows, P("groups")),
        check_vma=False,
    )
```

```python
import jax
import jax.numpy as jnp
from jax import lax
from jax.experimental import pallas as pl
from jax.experimental.pallas import tpu as pltpu
from jax.sharding import PartitionSpec as P

GROUP = ("wide", "narrow")
LANES = 128
VMEM = pl.BlockSpec(memory_space=pltpu.VMEM)
SMEM = pl.BlockSpec(memory_space=pltpu.SMEM)
HBM = pl.BlockSpec(memory_space=pltpu.HBM)


def in_hbm(x):
    return pltpu.with_memory_space_constraint(x, pltpu.HBM)


def normalize(rows):
    values = rows.astype(jnp.float32)
    scales = lax.rsqrt(jnp.sum(values * values, axis=1, keepdims=True) + 1e-06)
    return (values * scales, scales)


def backnorm(unit, scales, grad_unit):
    return scales * (grad_unit - unit * jnp.sum(unit * grad_unit, axis=1, keepdims=True))


def pair_terms(cosine, logit, matched):
    against = jnp.where(matched, -logit, logit)
    small = jnp.exp(-jnp.abs(logit))
    loss = jnp.maximum(against, 0.0) + jnp.log1p(small)
    sigma = jnp.where(against >= 0.0, 1.0, small) / (1.0 + small)
    return loss, jnp.where(matched, -sigma, sigma)


def pack_kernel(mates_hbm, img_hbm, txt_hbm, out_ref, mates_ref, mates_sem, sems):
    rows, width = img_hbm.shape
    copies = [
        pltpu.make_async_copy(source, out_ref.at[:, i * width : (i + 1) * width], sems.at[i])
        for i, source in enumerate((img_hbm, txt_hbm))
    ]
    indices = pltpu.make_async_copy(mates_hbm, mates_ref, mates_sem)
    indices.start()
    for copy in copies:
        copy.start()
    indices.wait()
    row = lax.broadcasted_iota(jnp.int32, (rows, LANES), 0)
    mates = jnp.zeros((rows, LANES), jnp.int32)
    for r in range(rows):
        mates = jnp.where(row == r, mates_ref[r], mates)
    out_ref[:, 2 * width :] = mates.astype(jnp.float32).astype(jnp.bfloat16)
    for copy in copies:
        copy.wait()


def pair_kernel(held, narrow, scalars_ref, *refs):
    count = sum(len(origins) for origins in held)
    stacks, refs = refs[: len(held)], refs[len(held) :]
    image_out, text_out, summary_out = refs[:3]
    img_half, txt_half, mates, weights = refs[3:]
    rows, width = image_out.shape
    tiles = width // LANES
    total = rows * count
    me = lax.axis_index("wide") * narrow + lax.axis_index("narrow")

    def unit_tiles(tile, first):
        values = [tile(first + t).astype(jnp.float32) for t in range(tiles)]
        squares = values[0] * values[0]
        for v in values[1:]:
            squares = squares + v * v
        scales = lax.rsqrt(jnp.sum(squares, axis=1, keepdims=True) + 1e-06)
        return [v * scales for v in values], scales

    own = None
    for origins, stack in zip(held, stacks):
        for place, (sources, flip) in enumerate(origins):
            tile = lambda t: stack[place * rows : (place + 1) * rows, t * LANES : (t + 1) * LANES]
            origin = jnp.int32(sources[0])
            for z, source in enumerate(sources[1:], 1):
                origin = jnp.where(me // narrow == z, source, origin)
            slot = origin * narrow + ((me % narrow) ^ flip)
            here = pl.ds(pl.multiple_of(slot * rows, rows), rows)
            img_units, img_scale = unit_tiles(tile, 0)
            txt_units, txt_scale = unit_tiles(tile, tiles)
            for t in range(tiles):
                lanes = slice(t * LANES, (t + 1) * LANES)
                img_half[here, lanes] = img_units[t].astype(jnp.bfloat16)
                txt_half[here, lanes] = txt_units[t].astype(jnp.bfloat16)
            mates[here, :] = tile(2 * tiles).astype(jnp.float32)
            if own is None:
                own = (img_units, img_scale, txt_units, txt_scale)

    nt = (((1,), (1,)), ((), ()))
    cosine = lax.dot_general(img_half[...], txt_half[...], nt, preferred_element_type=jnp.float32)
    sharp, shift = scalars_ref[0:1, :], scalars_ref[1:2, :]
    logit = sharp * cosine + shift
    column = lax.broadcasted_iota(jnp.int32, (total, LANES), 1).astype(jnp.float32)
    matched = jnp.concatenate(
        [mates[...] == column + float(c * LANES) for c in range(total // LANES)], axis=1
    )
    loss, slope = pair_terms(cosine, logit, matched)
    weights[...] = (sharp * slope).astype(jnp.bfloat16)
    summary_out[0] = jnp.sum(loss) / total
    summary_out[1] = jnp.sum(slope * cosine)
    summary_out[2] = jnp.sum(slope)

    mine = pl.ds(pl.multiple_of(me * rows, rows), rows)
    first_lane = (lax.broadcasted_iota(jnp.int32, (rows, LANES), 1) == 0).astype(jnp.float32)
    partner = lax.dot_general(
        first_lane.astype(jnp.bfloat16),
        mates[...].astype(jnp.bfloat16),
        nt,
        preferred_element_type=jnp.float32,
    )
    own_text = lax.broadcasted_iota(jnp.int32, (rows, total), 0) + me * rows
    turned = lax.dot_general(
        txt_half[mine, :], img_half[...], nt, preferred_element_type=jnp.float32
    )
    turned_slope = pair_terms(
        turned, sharp * turned + shift, partner == own_text.astype(jnp.float32)
    )[1]
    text_weights = (sharp * turned_slope).astype(jnp.bfloat16)
    img_grad = jnp.dot(weights[mine, :], txt_half[...], preferred_element_type=jnp.float32)
    txt_grad = jnp.dot(text_weights, img_half[...], preferred_element_type=jnp.float32)

    def store(out, units, scale, grad):
        parts = [grad[:, t * LANES : (t + 1) * LANES] for t in range(tiles)]
        along = units[0] * parts[0]
        for u, g in zip(units[1:], parts[1:]):
            along = along + u * g
        along = jnp.sum(along, axis=1, keepdims=True)
        for t in range(tiles):
            out[:, t * LANES : (t + 1) * LANES] = scale * (parts[t] - units[t] * along)

    store(image_out, own[0], own[1], img_grad)
    store(text_out, own[2], own[3], txt_grad)


def small_group(wide, narrow, images, texts, mates, sharpness, offset):
    rows, width = images.shape
    count = wide * narrow
    packed = pl.pallas_call(
        pack_kernel,
        out_shape=pltpu.VMEM((rows, 2 * width + LANES), jnp.bfloat16),
        in_specs=[HBM, HBM, HBM],
        out_specs=VMEM,
        scratch_shapes=[
            pltpu.SMEM((rows,), jnp.int32),
            pltpu.SemaphoreType.DMA,
            pltpu.SemaphoreType.DMA((2,)),
        ],
    )(*(in_hbm(x) for x in (mates, images, texts)))

    def swap(x, distance):
        return lax.ppermute(x, GROUP, [(i, i ^ distance) for i in range(count)])

    total = rows * count
    scalars = jnp.stack([jnp.broadcast_to(v, (total,)) for v in (sharpness, offset)])

    def join(*parts):
        return tuple(d for ds, _ in parts for d in ds), jnp.concatenate([p for _, p in parts])

    def turned(part, sources):
        pairs = [(sources[z] * narrow + n, z * narrow + n) for z in range(wide) for n in range(narrow)]
        return tuple((sources, f) for _, f in part[0]), lax.ppermute(part[1], GROUP, pairs)

    def send(part, flip):
        return tuple((s, f ^ flip) for s, f in part[0]), swap(part[1], flip)

    chip, core = 2, 1
    own = (((tuple(range(wide)), 0),), packed)
    first = turned(own, (3, 2, 0, 1))
    third = turned(own, (2, 3, 1, 0))
    near = turned(own, (1, 0, 3, 2))
    early, late = join(own, first), join(near, third)
    blocks, scalars = lax.optimization_barrier((early[1], scalars))
    early = (early[0], blocks)
    xearly, xlate = send(early, chip), send(late, chip)
    held = [early, late, xearly, xlate]
    held += [send(h, core) for h in held]

    kernel = lambda *refs: pair_kernel([d for d, _ in held], narrow, *refs)
    return pl.pallas_call(
        kernel,
        out_shape=(
            jax.ShapeDtypeStruct((rows, width), jnp.float32),
            jax.ShapeDtypeStruct((rows, width), jnp.float32),
            jax.ShapeDtypeStruct((3,), jnp.float32),
        ),
        in_specs=[VMEM] * (1 + len(held)),
        out_specs=(VMEM, VMEM, SMEM),
        scratch_shapes=[
            pltpu.VMEM((total, width), jnp.bfloat16),
            pltpu.VMEM((total, width), jnp.bfloat16),
            pltpu.VMEM((total, LANES), jnp.float32),
            pltpu.VMEM((total, total), jnp.bfloat16),
        ],
        compiler_params=pltpu.CompilerParams(vmem_limit_bytes=32 * 1024 * 1024),
    )(scalars, *[part for _, part in held])


def any_group(wide, narrow, images, texts, mates, sharpness, offset):
    rows = images.shape[0]
    total = rows * wide * narrow
    first = (lax.axis_index("wide") * narrow + lax.axis_index("narrow")) * rows
    unit_img, inv_img = normalize(images)
    unit_txt, inv_txt = normalize(texts)
    img_half, txt_half = unit_img.astype(jnp.bfloat16), unit_txt.astype(jnp.bfloat16)
    all_img = lax.all_gather(img_half, GROUP, axis=0, tiled=True)
    all_txt = lax.all_gather(txt_half, GROUP, axis=0, tiled=True)
    all_mates = lax.all_gather(mates, GROUP, axis=0, tiled=True)
    sharp, shift = sharpness[0], offset[0]

    def weigh(cosine, matched):
        loss, slope = pair_terms(cosine, sharp * cosine + shift, matched)
        return loss, slope, (sharp * slope).astype(jnp.bfloat16)

    here = first + jnp.arange(rows, dtype=jnp.int32)
    there = jnp.arange(total, dtype=jnp.int32)
    cosine = jnp.dot(img_half, all_txt.T, preferred_element_type=jnp.float32)
    loss, slope, weighted = weigh(cosine, mates[:, None] == there[None, :])
    sums = jnp.stack([jnp.sum(loss) / total, jnp.sum(slope * cosine), jnp.sum(slope)])
    img_grad = jnp.dot(weighted, all_txt, preferred_element_type=jnp.float32)
    turned = jnp.dot(txt_half, all_img.T, preferred_element_type=jnp.float32)
    weighted = weigh(turned, all_mates[None, :] == here[:, None])[2]
    txt_grad = jnp.dot(weighted, all_img, preferred_element_type=jnp.float32)
    return (
        backnorm(unit_img, inv_img, img_grad),
        backnorm(unit_txt, inv_txt, txt_grad),
        lax.psum(sums, GROUP),
    )


def solution(mesh):
    wide, narrow = mesh.shape["wide"], mesh.shape["narrow"]

    def per_device(images, texts, mates, sharpness, offset):
        total = images.shape[0] * wide * narrow
        small = wide == 4 and narrow == 4 and total <= 256 and total % LANES == 0
        form = small_group if small else any_group
        return form(wide, narrow, images, texts, mates, sharpness, offset)

    rows = P(("groups", "wide", "narrow"))
    return jax.shard_map(
        per_device,
        mesh=mesh,
        in_specs=(rows, rows, rows, P(), P()),
        out_specs=(rows, rows, P("groups")),
        check_vma=False,
    )
```

```python
import jax
import jax.numpy as jnp
from jax import lax
from jax.experimental import pallas as pl
from jax.experimental.pallas import tpu as pltpu
from jax.sharding import PartitionSpec as P

GROUP = ("wide", "narrow")
LANES = 128
VMEM = pl.BlockSpec(memory_space=pltpu.VMEM)
SMEM = pl.BlockSpec(memory_space=pltpu.SMEM)
HBM = pl.BlockSpec(memory_space=pltpu.HBM)


def in_vmem(x):
    return pltpu.with_memory_space_constraint(x, pltpu.VMEM)


def in_hbm(x):
    return pltpu.with_memory_space_constraint(x, pltpu.HBM)


def normalize(rows):
    values = rows.astype(jnp.float32)
    scales = lax.rsqrt(jnp.sum(values * values, axis=1, keepdims=True) + 1e-06)
    return (values * scales, scales)


def backnorm(unit, scales, grad_unit):
    return scales * (grad_unit - unit * jnp.sum(unit * grad_unit, axis=1, keepdims=True))


def pair_terms(cosine, logit, matched):
    against = jnp.where(matched, -logit, logit)
    small = jnp.exp(-jnp.abs(logit))
    loss = jnp.maximum(against, 0.0) + jnp.log1p(small)
    sigma = jnp.where(against >= 0.0, 1.0, small) / (1.0 + small)
    return loss, jnp.where(matched, -sigma, sigma)


def pack_kernel(mates_hbm, img_hbm, txt_hbm, out_ref, mates_ref, mates_sem, sems):
    rows, width = img_hbm.shape
    copies = [
        pltpu.make_async_copy(source, out_ref.at[:, i * width : (i + 1) * width], sems.at[i])
        for i, source in enumerate((img_hbm, txt_hbm))
    ]
    indices = pltpu.make_async_copy(mates_hbm, mates_ref, mates_sem)
    indices.start()
    for copy in copies:
        copy.start()
    indices.wait()
    row = lax.broadcasted_iota(jnp.int32, (rows, LANES), 0)
    mates = jnp.zeros((rows, LANES), jnp.int32)
    for r in range(rows):
        mates = jnp.where(row == r, mates_ref[r], mates)
    out_ref[:, 2 * width :] = mates.astype(jnp.float32).astype(jnp.bfloat16)
    for copy in copies:
        copy.wait()


def unit_rows(block, tiles):
    parts = []
    for first in (0, tiles):
        values = [
            block[0 : block.shape[0] // 2, (first + t) * LANES : (first + t + 1) * LANES].astype(jnp.float32)
            for t in range(tiles)
        ]
        squares = values[0] * values[0]
        for v in values[1:]:
            squares = squares + v * v
        scales = lax.rsqrt(jnp.sum(squares, axis=1, keepdims=True) + 1e-06)
        parts += [[v * scales for v in values], scales]
    return parts


def place_blocks(held, stacks, img_half, txt_half, mates, me, rows, tiles):
    def unit_tiles(tile, first):
        values = [tile(first + t).astype(jnp.float32) for t in range(tiles)]
        squares = values[0] * values[0]
        for v in values[1:]:
            squares = squares + v * v
        scales = lax.rsqrt(jnp.sum(squares, axis=1, keepdims=True) + 1e-06)
        return [v * scales for v in values], scales

    first_block = None
    for origins, stack in zip(held, stacks):
        for place, slot in enumerate(origins):
            tile = lambda t: stack[place * rows : (place + 1) * rows, t * LANES : (t + 1) * LANES]
            here = pl.ds(pl.multiple_of(slot(me) * rows, rows), rows)
            img_units, img_scale = unit_tiles(tile, 0)
            txt_units, txt_scale = unit_tiles(tile, tiles)
            for t in range(tiles):
                lanes = slice(t * LANES, (t + 1) * LANES)
                img_half[here, lanes] = img_units[t].astype(jnp.bfloat16)
                txt_half[here, lanes] = txt_units[t].astype(jnp.bfloat16)
            mates[here, :] = tile(2 * tiles).astype(jnp.float32)
            if first_block is None:
                first_block = (img_units, img_scale, txt_units, txt_scale)
    return first_block


def early_kernel(held, narrow, rows, width, *refs):
    me = lax.axis_index("wide") * narrow + lax.axis_index("narrow")
    place_blocks(held, refs[: len(held)], *refs[len(held) :], me, rows, width // LANES)


def pair_kernel(held, count, narrow, scalars_ref, own_ref, *refs):
    stacks, refs = refs[: len(held)], refs[len(held) + 3 :]
    image_out, text_out, summary_out, img_half, txt_half, mates, weights = refs
    rows, width = image_out.shape
    tiles = width // LANES
    total = rows * count
    me = lax.axis_index("wide") * narrow + lax.axis_index("narrow")

    own = unit_rows(own_ref, tiles)
    place_blocks(held, stacks, img_half, txt_half, mates, me, rows, tiles)

    nt = (((1,), (1,)), ((), ()))
    cosine = lax.dot_general(img_half[...], txt_half[...], nt, preferred_element_type=jnp.float32)
    sharp, shift = scalars_ref[0:1, :], scalars_ref[1:2, :]
    logit = sharp * cosine + shift
    column = lax.broadcasted_iota(jnp.int32, (total, LANES), 1).astype(jnp.float32)
    matched = jnp.concatenate(
        [mates[...] == column + float(c * LANES) for c in range(total // LANES)], axis=1
    )
    loss, slope = pair_terms(cosine, logit, matched)
    weights[...] = (sharp * slope).astype(jnp.bfloat16)
    summary_out[0] = jnp.sum(loss) / total
    summary_out[1] = jnp.sum(slope * cosine)
    summary_out[2] = jnp.sum(slope)

    mine = pl.ds(pl.multiple_of(me * rows, rows), rows)
    first_lane = (lax.broadcasted_iota(jnp.int32, (rows, LANES), 1) == 0).astype(jnp.float32)
    partner = lax.dot_general(
        first_lane.astype(jnp.bfloat16),
        mates[...].astype(jnp.bfloat16),
        nt,
        preferred_element_type=jnp.float32,
    )
    own_text = lax.broadcasted_iota(jnp.int32, (rows, total), 0) + me * rows
    turned = lax.dot_general(
        txt_half[mine, :], img_half[...], nt, preferred_element_type=jnp.float32
    )
    turned_slope = pair_terms(
        turned, sharp * turned + shift, partner == own_text.astype(jnp.float32)
    )[1]
    text_weights = (sharp * turned_slope).astype(jnp.bfloat16)
    img_grad = jnp.dot(weights[mine, :], txt_half[...], preferred_element_type=jnp.float32)
    txt_grad = jnp.dot(text_weights, img_half[...], preferred_element_type=jnp.float32)

    def store(out, units, scale, grad):
        parts = [grad[:, t * LANES : (t + 1) * LANES] for t in range(tiles)]
        along = units[0] * parts[0]
        for u, g in zip(units[1:], parts[1:]):
            along = along + u * g
        along = jnp.sum(along, axis=1, keepdims=True)
        for t in range(tiles):
            out[:, t * LANES : (t + 1) * LANES] = scale * (parts[t] - units[t] * along)

    store(image_out, own[0], own[1], img_grad)
    store(text_out, own[2], own[3], txt_grad)


def small_group(wide, narrow, images, texts, mates, sharpness, offset):
    rows, width = images.shape
    count = wide * narrow
    packed = pl.pallas_call(
        pack_kernel,
        out_shape=pltpu.VMEM((rows, 2 * width + LANES), jnp.bfloat16),
        in_specs=[HBM, HBM, HBM],
        out_specs=VMEM,
        scratch_shapes=[
            pltpu.SMEM((rows,), jnp.int32),
            pltpu.SemaphoreType.DMA,
            pltpu.SemaphoreType.DMA((2,)),
        ],
    )(*(in_hbm(x) for x in (mates, images, texts)))

    def swap(x, distance):
        return lax.ppermute(x, GROUP, [(i, i ^ distance) for i in range(count)])

    total = rows * count
    scalars = jnp.stack([jnp.broadcast_to(v, (total,)) for v in (sharpness, offset)])
    chip, core = 2, 1
    stay = tuple(range(wide))

    def place(me, sources, flip):
        origin = jnp.int32(sources[0])
        for z, source in enumerate(sources[1:], 1):
            origin = jnp.where(me // narrow == z, source, origin)
        return origin * narrow + ((me % narrow) ^ flip)

    def slot(even_from, odd_from):
        return lambda me: jnp.where(me % 2 == 1, place(me, *odd_from), place(me, *even_from))

    def move(blocks, even_from, odd_from):
        pairs = []
        for z in range(wide):
            for n in range(narrow):
                sources, flip = odd_from if n % 2 else even_from
                pairs.append((sources[z] * narrow + (n ^ flip), z * narrow + n))
        return lax.ppermute(blocks, GROUP, pairs)

    def across(slots, blocks):
        return [lambda me, f=f: f(me ^ core) for f in slots], swap(blocks, core)

    even_from, odd_from = ((3, 2, 0, 1), (1, 0, 3, 2), (2, 3, 1, 0)), ((3, 2, 0, 1), (1, 0, 3, 2), (2, 3, 1, 0))
    froms = [((e, 0), (o, 0)) for e, o in zip(even_from, odd_from)]
    own_slot = slot((stay, 0), (stay, 0))
    first = move(packed, *froms[0])
    third = move(packed, *froms[2])
    near = move(packed, *froms[1])
    early, late = jnp.concatenate([packed, first]), jnp.concatenate([near, third])
    early, scalars = lax.optimization_barrier((early, scalars))
    pairs = [[own_slot, slot(*froms[0])], [slot(*froms[1]), slot(*froms[2])]]
    flipped = [[lambda me, f=f: f(me ^ chip) for f in p] for p in pairs]
    held = [(pairs[0], early), (pairs[1], late)]
    held += [(flipped[0], swap(early, chip)), (flipped[1], swap(late, chip))]
    held += [across(*part) for part in held]

    early_count = len(held) - 1
    halves = pl.pallas_call(
        lambda *refs: early_kernel([d for d, _ in held[:-1]], narrow, rows, width, *refs),
        out_shape=(
            pltpu.VMEM((total, width), jnp.bfloat16),
            pltpu.VMEM((total, width), jnp.bfloat16),
            pltpu.VMEM((total, LANES), jnp.float32),
        ),
        in_specs=[VMEM] * early_count,
        out_specs=(VMEM, VMEM, VMEM),
    )(*[in_vmem(part) for _, part in held[:-1]])
    last = held[-1:]
    return pl.pallas_call(
        lambda *refs: pair_kernel([d for d, _ in last], count, narrow, *refs),
        out_shape=(
            jax.ShapeDtypeStruct((rows, width), jnp.float32),
            jax.ShapeDtypeStruct((rows, width), jnp.float32),
            jax.ShapeDtypeStruct((3,), jnp.float32),
            pltpu.VMEM((total, width), jnp.bfloat16),
            pltpu.VMEM((total, width), jnp.bfloat16),
            pltpu.VMEM((total, LANES), jnp.float32),
        ),
        in_specs=[VMEM] * 6,
        out_specs=(VMEM, VMEM, SMEM, VMEM, VMEM, VMEM),
        input_output_aliases={3: 3, 4: 4, 5: 5},
        scratch_shapes=[pltpu.VMEM((total, total), jnp.bfloat16)],
        compiler_params=pltpu.CompilerParams(vmem_limit_bytes=32 * 1024 * 1024),
    )(scalars, in_vmem(held[0][1]), last[0][1], *[in_vmem(h) for h in halves])[:3]


def any_group(wide, narrow, images, texts, mates, sharpness, offset):
    rows = images.shape[0]
    total = rows * wide * narrow
    first = (lax.axis_index("wide") * narrow + lax.axis_index("narrow")) * rows
    unit_img, inv_img = normalize(images)
    unit_txt, inv_txt = normalize(texts)
    img_half, txt_half = unit_img.astype(jnp.bfloat16), unit_txt.astype(jnp.bfloat16)
    all_img = lax.all_gather(img_half, GROUP, axis=0, tiled=True)
    all_txt = lax.all_gather(txt_half, GROUP, axis=0, tiled=True)
    all_mates = lax.all_gather(mates, GROUP, axis=0, tiled=True)
    sharp, shift = sharpness[0], offset[0]

    def weigh(cosine, matched):
        loss, slope = pair_terms(cosine, sharp * cosine + shift, matched)
        return loss, slope, (sharp * slope).astype(jnp.bfloat16)

    here = first + jnp.arange(rows, dtype=jnp.int32)
    there = jnp.arange(total, dtype=jnp.int32)
    cosine = jnp.dot(img_half, all_txt.T, preferred_element_type=jnp.float32)
    loss, slope, weighted = weigh(cosine, mates[:, None] == there[None, :])
    sums = jnp.stack([jnp.sum(loss) / total, jnp.sum(slope * cosine), jnp.sum(slope)])
    img_grad = jnp.dot(weighted, all_txt, preferred_element_type=jnp.float32)
    turned = jnp.dot(txt_half, all_img.T, preferred_element_type=jnp.float32)
    weighted = weigh(turned, all_mates[None, :] == here[:, None])[2]
    txt_grad = jnp.dot(weighted, all_img, preferred_element_type=jnp.float32)
    return (
        backnorm(unit_img, inv_img, img_grad),
        backnorm(unit_txt, inv_txt, txt_grad),
        lax.psum(sums, GROUP),
    )


def solution(mesh):
    wide, narrow = mesh.shape["wide"], mesh.shape["narrow"]

    def per_device(images, texts, mates, sharpness, offset):
        total = images.shape[0] * wide * narrow
        small = wide == 4 and narrow == 4 and total <= 256 and total % LANES == 0
        form = small_group if small else any_group
        return form(wide, narrow, images, texts, mates, sharpness, offset)

    rows = P(("groups", "wide", "narrow"))
    return jax.shard_map(
        per_device,
        mesh=mesh,
        in_specs=(rows, rows, rows, P(), P()),
        out_specs=(rows, rows, P("groups")),
        check_vma=False,
    )
```

```python
import jax
import jax.numpy as jnp
from jax import lax
from jax.experimental import pallas as pl
from jax.experimental.pallas import tpu as pltpu
from jax.sharding import PartitionSpec as P

GROUP = ("wide", "narrow")
LANES = 128
VMEM = pl.BlockSpec(memory_space=pltpu.VMEM)
SMEM = pl.BlockSpec(memory_space=pltpu.SMEM)
HBM = pl.BlockSpec(memory_space=pltpu.HBM)


def in_vmem(x):
    return pltpu.with_memory_space_constraint(x, pltpu.VMEM)


def in_hbm(x):
    return pltpu.with_memory_space_constraint(x, pltpu.HBM)


def normalize(rows):
    values = rows.astype(jnp.float32)
    scales = lax.rsqrt(jnp.sum(values * values, axis=1, keepdims=True) + 1e-06)
    return (values * scales, scales)


def backnorm(unit, scales, grad_unit):
    return scales * (grad_unit - unit * jnp.sum(unit * grad_unit, axis=1, keepdims=True))


def pair_terms(cosine, logit, matched):
    against = jnp.where(matched, -logit, logit)
    small = jnp.exp(-jnp.abs(logit))
    loss = jnp.maximum(against, 0.0) + jnp.log1p(small)
    sigma = jnp.where(against >= 0.0, 1.0, small) / (1.0 + small)
    return loss, jnp.where(matched, -sigma, sigma)


def pack_kernel(mates_hbm, img_hbm, txt_hbm, out_ref, mates_ref, mates_sem, sems):
    rows, width = img_hbm.shape
    copies = [
        pltpu.make_async_copy(source, out_ref.at[:, i * width : (i + 1) * width], sems.at[i])
        for i, source in enumerate((img_hbm, txt_hbm))
    ]
    indices = pltpu.make_async_copy(mates_hbm, mates_ref, mates_sem)
    indices.start()
    for copy in copies:
        copy.start()
    indices.wait()
    row = lax.broadcasted_iota(jnp.int32, (rows, LANES), 0)
    mates = jnp.zeros((rows, LANES), jnp.int32)
    for r in range(rows):
        mates = jnp.where(row == r, mates_ref[r], mates)
    out_ref[:, 2 * width :] = mates.astype(jnp.float32).astype(jnp.bfloat16)
    for copy in copies:
        copy.wait()


def own_rows(units, scales, tiles):
    parts = []
    for i in range(2):
        first = i * tiles
        parts += [
            [units[:, (first + t) * LANES : (first + t + 1) * LANES] for t in range(tiles)],
            scales[:, i * LANES : (i + 1) * LANES],
        ]
    return parts


def place_blocks(held, stacks, img_half, txt_half, mates, me, rows, tiles):
    def unit_tiles(tile, first):
        values = [tile(first + t).astype(jnp.float32) for t in range(tiles)]
        squares = values[0] * values[0]
        for v in values[1:]:
            squares = squares + v * v
        scales = lax.rsqrt(jnp.sum(squares, axis=1, keepdims=True) + 1e-06)
        return [v * scales for v in values], scales

    first_block = None
    for origins, stack in zip(held, stacks):
        for place, slot in enumerate(origins):
            tile = lambda t: stack[place * rows : (place + 1) * rows, t * LANES : (t + 1) * LANES]
            here = pl.ds(pl.multiple_of(slot(me) * rows, rows), rows)
            img_units, img_scale = unit_tiles(tile, 0)
            txt_units, txt_scale = unit_tiles(tile, tiles)
            for t in range(tiles):
                lanes = slice(t * LANES, (t + 1) * LANES)
                img_half[here, lanes] = img_units[t].astype(jnp.bfloat16)
                txt_half[here, lanes] = txt_units[t].astype(jnp.bfloat16)
            mates[here, :] = tile(2 * tiles).astype(jnp.float32)
            if first_block is None:
                first_block = (img_units, img_scale, txt_units, txt_scale)
    return first_block


def early_kernel(held, narrow, rows, width, *refs):
    me = lax.axis_index("wide") * narrow + lax.axis_index("narrow")
    buffers, (units, scales) = refs[len(held) : len(held) + 3], refs[len(held) + 3 :]
    tiles = width // LANES
    own = place_blocks(held, refs[: len(held)], *buffers, me, rows, tiles)
    for i in range(2):
        for t in range(tiles):
            at = i * tiles + t
            units[:, at * LANES : (at + 1) * LANES] = own[2 * i][t]
        scales[:, i * LANES : (i + 1) * LANES] = jnp.broadcast_to(own[2 * i + 1], (rows, LANES))


def pair_kernel(held, count, narrow, scalars_ref, units_ref, scales_ref, *refs):
    stacks, refs = refs[: len(held)], refs[len(held) + 3 :]
    image_out, text_out, summary_out, img_half, txt_half, mates, weights = refs
    rows, width = image_out.shape
    tiles = width // LANES
    total = rows * count
    me = lax.axis_index("wide") * narrow + lax.axis_index("narrow")

    own = own_rows(units_ref, scales_ref, tiles)
    place_blocks(held, stacks, img_half, txt_half, mates, me, rows, tiles)

    nt = (((1,), (1,)), ((), ()))
    cosine = lax.dot_general(img_half[...], txt_half[...], nt, preferred_element_type=jnp.float32)
    sharp, shift = scalars_ref[0:1, :], scalars_ref[1:2, :]
    logit = sharp * cosine + shift
    column = lax.broadcasted_iota(jnp.int32, (total, LANES), 1).astype(jnp.float32)
    matched = jnp.concatenate(
        [mates[...] == column + float(c * LANES) for c in range(total // LANES)], axis=1
    )
    loss, slope = pair_terms(cosine, logit, matched)
    weights[...] = (sharp * slope).astype(jnp.bfloat16)
    summary_out[0] = jnp.sum(loss) / total
    summary_out[1] = jnp.sum(slope * cosine)
    summary_out[2] = jnp.sum(slope)

    mine = pl.ds(pl.multiple_of(me * rows, rows), rows)
    first_lane = (lax.broadcasted_iota(jnp.int32, (rows, LANES), 1) == 0).astype(jnp.float32)
    partner = lax.dot_general(
        first_lane.astype(jnp.bfloat16),
        mates[...].astype(jnp.bfloat16),
        nt,
        preferred_element_type=jnp.float32,
    )
    own_text = lax.broadcasted_iota(jnp.int32, (rows, total), 0) + me * rows
    turned = lax.dot_general(
        txt_half[mine, :], img_half[...], nt, preferred_element_type=jnp.float32
    )
    turned_slope = pair_terms(
        turned, sharp * turned + shift, partner == own_text.astype(jnp.float32)
    )[1]
    text_weights = (sharp * turned_slope).astype(jnp.bfloat16)
    img_grad = jnp.dot(weights[mine, :], txt_half[...], preferred_element_type=jnp.float32)
    txt_grad = jnp.dot(text_weights, img_half[...], preferred_element_type=jnp.float32)

    def store(out, units, scale, grad):
        parts = [grad[:, t * LANES : (t + 1) * LANES] for t in range(tiles)]
        along = units[0] * parts[0]
        for u, g in zip(units[1:], parts[1:]):
            along = along + u * g
        along = jnp.sum(along, axis=1, keepdims=True)
        for t in range(tiles):
            out[:, t * LANES : (t + 1) * LANES] = scale * (parts[t] - units[t] * along)

    store(image_out, own[0], own[1], img_grad)
    store(text_out, own[2], own[3], txt_grad)


def small_group(wide, narrow, images, texts, mates, sharpness, offset):
    rows, width = images.shape
    count = wide * narrow
    packed = pl.pallas_call(
        pack_kernel,
        out_shape=pltpu.VMEM((rows, 2 * width + LANES), jnp.bfloat16),
        in_specs=[HBM, HBM, HBM],
        out_specs=VMEM,
        scratch_shapes=[
            pltpu.SMEM((rows,), jnp.int32),
            pltpu.SemaphoreType.DMA,
            pltpu.SemaphoreType.DMA((2,)),
        ],
    )(*(in_hbm(x) for x in (mates, images, texts)))

    def swap(x, distance):
        return lax.ppermute(x, GROUP, [(i, i ^ distance) for i in range(count)])

    total = rows * count
    scalars = jnp.stack([jnp.broadcast_to(v, (total,)) for v in (sharpness, offset)])
    chip, core = 2, 1
    stay = tuple(range(wide))

    def place(me, sources, flip):
        origin = jnp.int32(sources[0])
        for z, source in enumerate(sources[1:], 1):
            origin = jnp.where(me // narrow == z, source, origin)
        return origin * narrow + ((me % narrow) ^ flip)

    def slot(even_from, odd_from):
        return lambda me: jnp.where(me % 2 == 1, place(me, *odd_from), place(me, *even_from))

    def move(blocks, even_from, odd_from):
        pairs = []
        for z in range(wide):
            for n in range(narrow):
                sources, flip = odd_from if n % 2 else even_from
                pairs.append((sources[z] * narrow + (n ^ flip), z * narrow + n))
        return lax.ppermute(blocks, GROUP, pairs)

    def across(slots, blocks):
        return [lambda me, f=f: f(me ^ core) for f in slots], swap(blocks, core)

    even_from, odd_from = ((3, 2, 0, 1), (1, 0, 3, 2), (2, 3, 1, 0)), ((2, 3, 0, 1), (1, 0, 3, 2), (3, 2, 1, 0))
    froms = [((e, 0), (o, 0)) for e, o in zip(even_from, odd_from)]
    own_slot = slot((stay, 0), (stay, 0))
    first = move(packed, *froms[0])
    third = move(packed, *froms[2])
    near = move(packed, *froms[1])
    early, late = jnp.concatenate([packed, first]), jnp.concatenate([near, third])
    pairs = [[own_slot, slot(*froms[0])], [slot(*froms[1]), slot(*froms[2])]]
    flipped = [[lambda me, f=f: f(me ^ chip) for f in p] for p in pairs]
    held = [(pairs[0], early), (pairs[1], late)]
    xearly, xlate = swap(early, chip), swap(late, chip)
    xearly, scalars = lax.optimization_barrier((xearly, scalars))
    held += [(flipped[0], xearly), (flipped[1], xlate)]
    held += [across(*part) for part in held]

    early_count = len(held) - 1
    *halves, units, scales = pl.pallas_call(
        lambda *refs: early_kernel([d for d, _ in held[:-1]], narrow, rows, width, *refs),
        out_shape=(
            pltpu.VMEM((total, width), jnp.bfloat16),
            pltpu.VMEM((total, width), jnp.bfloat16),
            pltpu.VMEM((total, LANES), jnp.float32),
            pltpu.VMEM((rows, 2 * width), jnp.float32),
            pltpu.VMEM((rows, 2 * LANES), jnp.float32),
        ),
        in_specs=[VMEM] * early_count,
        out_specs=(VMEM,) * 5,
    )(*[in_vmem(part) for _, part in held[:-1]])
    last = held[-1:]
    return pl.pallas_call(
        lambda *refs: pair_kernel([d for d, _ in last], count, narrow, *refs),
        out_shape=(
            jax.ShapeDtypeStruct((rows, width), jnp.float32),
            jax.ShapeDtypeStruct((rows, width), jnp.float32),
            jax.ShapeDtypeStruct((3,), jnp.float32),
            pltpu.VMEM((total, width), jnp.bfloat16),
            pltpu.VMEM((total, width), jnp.bfloat16),
            pltpu.VMEM((total, LANES), jnp.float32),
        ),
        in_specs=[VMEM] * 7,
        out_specs=(VMEM, VMEM, SMEM, VMEM, VMEM, VMEM),
        input_output_aliases={4: 3, 5: 4, 6: 5},
        scratch_shapes=[pltpu.VMEM((total, total), jnp.bfloat16)],
        compiler_params=pltpu.CompilerParams(vmem_limit_bytes=32 * 1024 * 1024),
    )(scalars, in_vmem(units), in_vmem(scales), last[0][1], *[in_vmem(h) for h in halves])[:3]


def any_group(wide, narrow, images, texts, mates, sharpness, offset):
    rows = images.shape[0]
    total = rows * wide * narrow
    first = (lax.axis_index("wide") * narrow + lax.axis_index("narrow")) * rows
    unit_img, inv_img = normalize(images)
    unit_txt, inv_txt = normalize(texts)
    img_half, txt_half = unit_img.astype(jnp.bfloat16), unit_txt.astype(jnp.bfloat16)
    all_img = lax.all_gather(img_half, GROUP, axis=0, tiled=True)
    all_txt = lax.all_gather(txt_half, GROUP, axis=0, tiled=True)
    all_mates = lax.all_gather(mates, GROUP, axis=0, tiled=True)
    sharp, shift = sharpness[0], offset[0]

    def weigh(cosine, matched):
        loss, slope = pair_terms(cosine, sharp * cosine + shift, matched)
        return loss, slope, (sharp * slope).astype(jnp.bfloat16)

    here = first + jnp.arange(rows, dtype=jnp.int32)
    there = jnp.arange(total, dtype=jnp.int32)
    cosine = jnp.dot(img_half, all_txt.T, preferred_element_type=jnp.float32)
    loss, slope, weighted = weigh(cosine, mates[:, None] == there[None, :])
    sums = jnp.stack([jnp.sum(loss) / total, jnp.sum(slope * cosine), jnp.sum(slope)])
    img_grad = jnp.dot(weighted, all_txt, preferred_element_type=jnp.float32)
    turned = jnp.dot(txt_half, all_img.T, preferred_element_type=jnp.float32)
    weighted = weigh(turned, all_mates[None, :] == here[:, None])[2]
    txt_grad = jnp.dot(weighted, all_img, preferred_element_type=jnp.float32)
    return (
        backnorm(unit_img, inv_img, img_grad),
        backnorm(unit_txt, inv_txt, txt_grad),
        lax.psum(sums, GROUP),
    )


def solution(mesh):
    wide, narrow = mesh.shape["wide"], mesh.shape["narrow"]

    def per_device(images, texts, mates, sharpness, offset):
        total = images.shape[0] * wide * narrow
        small = wide == 4 and narrow == 4 and total <= 256 and total % LANES == 0
        form = small_group if small else any_group
        return form(wide, narrow, images, texts, mates, sharpness, offset)

    rows = P(("groups", "wide", "narrow"))
    return jax.shard_map(
        per_device,
        mesh=mesh,
        in_specs=(rows, rows, rows, P(), P()),
        out_specs=(rows, rows, P("groups")),
        check_vma=False,
    )
```
